256 devices in a mesh: wide: 32 (over x, z_lo, y), narrow: 8 (over z_hi, core).
Axes of the slice: x: 4, y: 4, z: 8 (z_hi: 4, z_lo: 2; z = z_hi * 2 + z_lo), core: 2. Of those that a mesh axis runs over, the one named last changes fastest.
Arguments:
- amplitudes: float32 [2048, 24576], P('narrow', 'wide'), may hold values from -6 to 6
- integrals: float32 [24576, 2, 8192], P('wide', None, 'narrow'), may hold values from -0.109375 to 0.109375
- ab_sizes: int32 [8], replicated, may hold values from 1 to 6144, 24576 in all
- cd_sizes: int32 [2, 8], replicated, may hold values from 1 to 2048, 8192 in all within a row
Outputs:
- ladder: float32 [2048, 2, 8192], P('wide', None, 'narrow')
The draws below stay inside these ranges and needn't reach their ends.
Inputs may be any that keep to these rules, and one draw needn't show every extreme that they name: `ab_sizes`: each entry is at least 1 and the entries sum to 24576; the largest is exactly 6144. `cd_sizes`: each row's entries are at least 1 and sum to 8192; the largest of each row is exactly 2048.
All inputs are finite; a program needn't handle non-finite values.
Results may differ from the reference program's by a relative error of at most 0.0003.
Values sent between devices are 32-bit elements; how exact they have to be, the bound alone decides.
A program may use at most 128 MiB of HBM per device.

```python
import math
import jax
import jax.numpy as jnp
import numpy as np
from jax import lax

IJ = 2048
IRREPS = 8
SLABS = 2
AB = 24576
CDS = 8192


def with_spikes(array, rng, source, target, parts, factor):
    owner, partner = [(jnp.arange(array.shape[axis_at]) // (array.shape[axis_at] // parts)).reshape([-1 if axis == axis_at else 1 for axis in range(array.ndim)]) for axis_at in (source, target)]
    chosen = jax.random.permutation(rng, parts)[partner]
    strong = (owner == chosen) | (owner == (partner + parts // 2) % parts)
    return jnp.where(strong, factor * array, array)


def block_scale(own_key, shape, cuts, low, high):
    def one(position, shards_of):
        draws = jax.random.uniform(jax.random.fold_in(jax.random.fold_in(own_key, 6), position), (shards_of,), jnp.float32, low / len(cuts), high / len(cuts))
        return jnp.repeat(jnp.exp(draws), shape[position] // shards_of).reshape((-1,) + (1,) * (len(shape) - position - 1))

    level = one(*cuts[0])
    for cut in cuts[1:]:
        level = level * one(*cut)
    return level


def profile(number_of, total, limit, slope):
    portions = [(1 << 20) // math.isqrt(grade ** slope) + 1 for grade in range(2, number_of + 1)]
    spare, counts = total - limit - (number_of - 1), [1] * (number_of - 1)
    while spare > 0:
        free = [i for i in range(number_of - 1) if counts[i] < limit]
        whole, left = sum([portions[i] for i in free]), spare
        for i in free:
            more = min(limit - counts[i], max(1, left * portions[i] // whole), spare)
            counts[i] = counts[i] + more
            spare = spare - more
    return np.array([limit] + counts)


def ragged(rng, amount, total, reach, slope):
    if amount == 2:
        one = jax.random.randint(rng, (), max(1, total - reach), min(reach, total - 1) + 1)
        return jnp.stack([one, total - one])
    tallies = jnp.asarray(profile(amount, total, reach, slope), jnp.int32)
    twos = (amount - 1) // 2
    donor, sink = tallies[1:1 + 2 * twos:2], tallies[2:2 + 2 * twos:2]
    slack = jnp.minimum(donor - 1, reach - sink)
    passed = jax.random.randint(jax.random.fold_in(rng, 1), (twos,), 0, 1 << 20) % (slack + 1)
    tallies = tallies.at[1:1 + 2 * twos:2].set(donor - passed).at[2:2 + 2 * twos:2].set(sink + passed)
    return tallies[jax.random.permutation(jax.random.fold_in(rng, 2), amount)]


def noise(rng, extent, width, most, shards=(), kind=jnp.bfloat16):
    entries = width * jax.random.normal(rng, extent, jnp.float32)
    if shards:
        entries = entries * block_scale(rng, extent, shards, -0.22, 0.18)
    return jnp.clip(entries, -most, most).astype(kind)


def noise_with(rng, extent, deviation, bound, shards, heavy, kind=jnp.bfloat16):
    result = deviation * jax.random.normal(rng, extent, jnp.float32)
    if shards:
        result = result * block_scale(rng, extent, shards, -0.22, 0.18)
    return jnp.clip(with_spikes(result, jax.random.fold_in(rng, 3), *heavy), -bound, bound).astype(kind)


def setup_inputs(seed: int = 0) -> dict:
    arg_keys = jax.random.split(jax.random.key(seed), 5)
    amplitudes = noise_with(arg_keys[0], (IJ, AB), 1.0, 6.0, ((0, 8), (1, 32)), (1, 0, 32, 2.75), jnp.float32)
    integrals = noise(arg_keys[1], (AB, SLABS, CDS), (AB // 8) ** -0.5, 0.109375, ((0, 32), (2, 8)), jnp.float32)
    ab_sizes = ragged(arg_keys[2], IRREPS, AB, AB // 4, 2).astype(jnp.int32)
    cd_sizes = jax.vmap(lambda own: ragged(own, IRREPS, CDS, CDS // 4, 2))(jax.random.split(arg_keys[3], SLABS)).reshape((SLABS, IRREPS)).astype(jnp.int32)
    return dict(amplitudes=amplitudes, integrals=integrals, ab_sizes=ab_sizes, cd_sizes=cd_sizes)


def irrep_labels(positions, sizes):
    block_ends = jnp.cumsum(sizes, axis=-1).astype(jnp.int32)
    return jnp.sum((positions[..., None] >= block_ends).astype(jnp.int32), axis=-1).astype(jnp.int32)


def reference(amplitudes, integrals, ab_sizes, cd_sizes):
    ab_label = irrep_labels(jnp.arange(AB, dtype=jnp.int32), ab_sizes)
    cd_positions = jnp.arange(CDS, dtype=jnp.int32)

    def one_slab(slab_index):
        slab_sizes = lax.dynamic_index_in_dim(cd_sizes, slab_index, 0, keepdims=False)
        cd_label = irrep_labels(cd_positions, slab_sizes)
        slab_tile = lax.dynamic_index_in_dim(integrals, slab_index, 1, keepdims=False)
        masked = jnp.where(ab_label[:, None] == cd_label[None, :], slab_tile, jnp.zeros((), slab_tile.dtype))
        return jnp.dot(amplitudes, masked, precision=lax.Precision.HIGHEST, preferred_element_type=jnp.float32)

    slabs_out = lax.map(one_slab, jnp.arange(SLABS, dtype=jnp.int32))
    return jnp.transpose(slabs_out, (1, 0, 2))
```

```python
import jax
import jax.numpy as jnp
from jax import lax
from jax.experimental import pallas as pl
from jax.experimental.pallas import tpu as pltpu
from jax.sharding import PartitionSpec as P

MESH = pl.DeviceIdType.MESH


def irrep_labels(positions, sizes):
    block_ends = jnp.cumsum(sizes, axis=-1)
    return jnp.sum((positions[..., None] >= block_ends).astype(jnp.int32), axis=-1)


def ladder_kernel(
    a_ref, bh_ref, bl_ref, out_ref, aall, ahl, p, yr, land, a_s, a_r, y_s, y_r, d_s, d_r
):
    rows, depth = a_ref.shape
    sub = rows // 4
    half = rows // 2
    cols = bh_ref.shape[2]
    w = lax.axis_index("wide")
    n = lax.axis_index("narrow")
    y = lax.rem(w, 4)
    j = lax.div(w, 4)
    x = lax.div(j, 2)
    zl = lax.rem(j, 2)
    zh = lax.div(n, 2)
    c = lax.rem(n, 2)
    right = (j * 4 + lax.rem(y + 1, 4), n)
    left = (j * 4 + lax.rem(y + 3, 4), n)
    zup = (w, lax.rem(zh + 1, 4) * 2 + c)
    zdn = (w, lax.rem(zh + 3, 4) * 2 + c)
    sib = (w, zh * 2 + 1 - c)

    def owner(d):
        return (lax.rem(j + d, 8) * 4 + y, n)

    barrier = pltpu.get_barrier_semaphore()
    for dev in [right, left, zup, zdn, sib] + [owner(d) for d in range(1, 8)]:
        pl.semaphore_signal(barrier, inc=1, device_id=dev, device_id_type=MESH)
    pl.semaphore_wait(barrier, 12)

    def remote(src, dst, ss, rs, dev):
        return pltpu.make_async_remote_copy(
            src_ref=src, dst_ref=dst, send_sem=ss, recv_sem=rs,
            device_id=dev, device_id_type=MESH,
        )

    lo, hi = pl.ds(0, half), pl.ds(half, half)

    def acopy(i):
        src, dst, dev = [
            (a_ref.at[lo], aall.at[0, 3, lo], zup),
            (a_ref.at[hi], aall.at[0, 3, hi], zup),
            (a_ref.at[hi], aall.at[0, 1, hi], zdn),
            (a_ref.at[lo], aall.at[0, 1, lo], zdn),
            (a_ref, aall.at[1, 0], sib),
            (aall.at[0, 3, lo], aall.at[0, 2, lo], zup),
            (aall.at[0, 1, hi], aall.at[0, 2, hi], zdn),
            (aall.at[0, 3], aall.at[1, 3], sib),
            (aall.at[0, 1], aall.at[1, 1], sib),
            (aall.at[0, 2], aall.at[1, 2], sib),
        ][i]
        return remote(src, dst, a_s.at[i], a_r.at[i], dev)

    for i in (4, 0, 2, 1, 3):
        acopy(i).start()
    aall[0, 0] = a_ref[...]

    r_own = lax.rem(x - zh + 4, 4)
    r_last = jnp.where(r_own == 0, 2, r_own)
    r_first = jnp.where(r_own == 1, 3, 1)
    r_mid = 6 - r_last - r_first
    q_last = jnp.where(c == zl, 0, 1)

    def slot(k):
        g = lax.div(k, 2)
        b = lax.rem(k, 2)
        r = jnp.where(g == 0, 0, jnp.where(g == 1, r_first, jnp.where(g == 2, r_mid, r_last)))
        q = jnp.where(g == 0, b, jnp.where(b == 1, q_last, 1 - q_last))
        return r, q

    def distance(k):
        r, q = slot(k)
        block = 2 * lax.rem(zh + r, 4) + jnp.where(q == 0, c, 1 - c)
        return lax.rem(block - j + 8, 8)

    def ring(s, t, k):
        at = lax.rem(y + 3 - t + 4, 4) if s == 0 else lax.rem(y + 1 + t, 4)
        piece = pl.ds(pl.multiple_of(at * sub, sub), sub)
        return piece, remote(
            p.at[s, k, piece], yr.at[s, t, k], y_s.at[s, t, k], y_r.at[s, t, k],
            right if s == 0 else left,
        )

    mine = pl.ds(pl.multiple_of(y * sub, sub), sub)

    def direct(k, d):
        return remote(p.at[:, k, mine], land.at[d], d_s.at[d], d_r.at[d], owner(d))

    def pass_on(t, k):
        for s in range(2):
            ring(s, t - 1, k)[1].wait_recv()
            piece, copy = ring(s, t, k)
            p[s, k, piece, :] += yr[s, t - 1, k]
            copy.start()

    def finish(k):
        for s in range(2):
            ring(s, 2, k)[1].wait_recv()
            p[s, k, mine, :] += yr[s, 2, k]
        d = distance(k)

        @pl.when(d != 0)
        def _():
            direct(k, d).start()

    def compute(k):
        r, q = slot(k)
        a = aall[q, r]
        ah = a.astype(jnp.bfloat16)
        ahl[0:rows] = ah
        ahl[rows:] = (a - ah.astype(jnp.float32)).astype(jnp.bfloat16)
        width = 512
        per = cols // width
        for s in range(2):
            def tile(ci, _):
                cs = pl.ds(pl.multiple_of(ci * width, width), width)
                u = jnp.dot(ahl[...], bh_ref[s, :, cs], preferred_element_type=jnp.float32)
                v = jnp.dot(ahl[0:rows], bl_ref[s, :, cs], preferred_element_type=jnp.float32)
                p[s, k, :, cs] = u[:rows] + (u[rows:] + v)
                return 0

            lax.fori_loop(0, per, tile, 0)
            ring(s, 0, k)[1].start()

    def body(i, _):
        @pl.when(i >= 3)
        def _():
            finish(i - 3)

        @pl.when((i >= 2) & (i < 10))
        def _():
            pass_on(2, i - 2)

        @pl.when((i >= 1) & (i < 9))
        def _():
            pass_on(1, i - 1)

        @pl.when(i == 1)
        def _():
            acopy(4).wait_recv()

        @pl.when(i == 2)
        def _():
            acopy(0).wait_recv()
            acopy(5).start()
            acopy(2).wait_recv()
            acopy(6).start()
            acopy(1).wait_recv()
            acopy(7).start()
            acopy(3).wait_recv()
            acopy(8).start()
            acopy(7).wait_recv()
            acopy(8).wait_recv()

        @pl.when(i == 4)
        def _():
            acopy(5).wait_recv()
            acopy(6).wait_recv()
            acopy(9).start()
            acopy(9).wait_recv()

        @pl.when(i < 8)
        def _():
            compute(i)

        return 0

    lax.fori_loop(0, 11, body, 0)

    k_own = 0
    for k in range(8):
        k_own = k_own + jnp.where(distance(k) == 0, k, 0)
    out_ref[...] = p[:, k_own, mine, :]
    for d in range(1, 8):
        direct(0, d).wait_recv()
        out_ref[...] += land[d]
    for d in range(1, 8):
        direct(0, d).wait_send()
    for i in range(10):
        acopy(i).wait_send()

    def drain(k, _):
        for s in range(2):
            for t in range(3):
                ring(s, t, k)[1].wait_send()
        return 0

    lax.fori_loop(0, 8, drain, 0)


def shards(amplitudes, integrals, ab_sizes, cd_sizes):
    pair_rows, slab_count, slab_cols = integrals.shape
    block = amplitudes.shape[0]
    ab_positions = lax.axis_index("wide") * pair_rows + lax.iota(jnp.int32, pair_rows)
    cd_positions = lax.axis_index("narrow") * slab_cols + lax.iota(jnp.int32, slab_cols)
    ab_label = irrep_labels(ab_positions, ab_sizes)
    cd_label = irrep_labels(cd_positions[None, :], cd_sizes[:, None, :])
    masked = jnp.where(
        ab_label[None, :, None] == cd_label[:, None, :],
        jnp.transpose(integrals, (1, 0, 2)),
        jnp.zeros((), integrals.dtype),
    )
    top = lax.reduce_precision(masked, 8, 7)
    high = top.astype(jnp.bfloat16)
    low = (masked - top).astype(jnp.bfloat16)
    f32 = jnp.float32
    vmem = pl.BlockSpec(memory_space=pltpu.VMEM)
    result = pl.pallas_call(
        ladder_kernel,
        out_shape=jax.ShapeDtypeStruct((slab_count, block // 4, slab_cols), f32),
        in_specs=[vmem] * 3,
        out_specs=vmem,
        scratch_shapes=[
            pltpu.VMEM((2, 4, block, pair_rows), f32),
            pltpu.VMEM((2 * block, pair_rows), jnp.bfloat16),
            pltpu.VMEM((2, 8, block, slab_cols), f32),
            pltpu.VMEM((2, 3, 8, block // 4, slab_cols), f32),
            pltpu.VMEM((8, 2, block // 4, slab_cols), f32),
            pltpu.SemaphoreType.DMA((10,)),
            pltpu.SemaphoreType.DMA((10,)),
            pltpu.SemaphoreType.DMA((2, 3, 8)),
            pltpu.SemaphoreType.DMA((2, 3, 8)),
            pltpu.SemaphoreType.DMA((8,)),
            pltpu.SemaphoreType.DMA((8,)),
        ],
        compiler_params=pltpu.CompilerParams(
            collective_id=0, has_side_effects=True, vmem_limit_bytes=60 * 2**20
        ),
        cost_estimate=pl.CostEstimate(
            flops=6 * 2048 * 768 * 2048, bytes_accessed=16 * 2**20, transcendentals=0
        ),
    )(amplitudes, high, low)
    return jnp.transpose(result, (1, 0, 2))


def solution(mesh):
    return jax.shard_map(
        shards,
        mesh=mesh,
        in_specs=(P("narrow", "wide"), P("wide", None, "narrow"), P(), P()),
        out_specs=P("wide", None, "narrow"),
        check_vma=False,
    )
```

```python
import jax
import jax.numpy as jnp
from jax import lax
from jax.experimental import pallas as pl
from jax.experimental.pallas import tpu as pltpu
from jax.sharding import PartitionSpec as P

MESH = pl.DeviceIdType.MESH
LANES = 128
SIDE = 256


def ladder_kernel(
    a_ref, b_hbm, ab_ref, cd_ref, out_ref,
    aall, ahl, braw, bh, bl, rowlab, py, px, yr, land, xl, zl2,
    b_sem, a_s, a_r, y_s, y_r, d_s, d_r, x_s, x_r, z_s, z_r,
):
    rows, depth = a_ref.shape
    sub = rows // 4
    half = rows // 2
    cols = bh.shape[2]
    main = cols - SIDE
    tiles = cols // LANES
    w = lax.axis_index("wide")
    n = lax.axis_index("narrow")
    y = lax.rem(w, 4)
    j = lax.div(w, 4)
    x = lax.div(j, 2)
    zl = lax.rem(j, 2)
    zh = lax.div(n, 2)
    c = lax.rem(n, 2)
    right = (j * 4 + lax.rem(y + 1, 4), n)
    left = (j * 4 + lax.rem(y + 3, 4), n)
    zup = (w, lax.rem(zh + 1, 4) * 2 + c)
    zdn = (w, lax.rem(zh + 3, 4) * 2 + c)
    sib = (w, zh * 2 + 1 - c)

    def owner(d):
        return (lax.rem(j + d, 8) * 4 + y, n)

    def plane(eb, dy):
        return ((2 * x + lax.rem(zl + eb, 2)) * 4 + lax.rem(y + dy, 4), n)

    load_b = pltpu.make_async_copy(b_hbm, braw, b_sem)
    load_b.start()

    partners = [right, left, zup, zdn, sib, plane(0, 2)]
    partners += [owner(d) for d in range(1, 8)] + [plane(1, dy) for dy in range(1, 4)]
    barrier = pltpu.get_barrier_semaphore()
    for dev in partners:
        pl.semaphore_signal(barrier, inc=1, device_id=dev, device_id_type=MESH)
    pl.semaphore_wait(barrier, len(partners))

    def remote(src, dst, ss, rs, dev):
        return pltpu.make_async_remote_copy(
            src_ref=src, dst_ref=dst, send_sem=ss, recv_sem=rs,
            device_id=dev, device_id_type=MESH,
        )

    hc = pl.ds(pl.multiple_of(c * half, half), half)

    def acopy(i):
        src, dst, dev = [
            (a_ref, aall.at[0, c], sib),
            (aall.at[0, 0, hc], aall.at[3, 0, hc], zup),
            (aall.at[0, 1, hc], aall.at[3, 1, hc], zup),
            (aall.at[3, 0, hc], aall.at[2, 0, hc], zup),
            (aall.at[0, 1, hc], aall.at[1, 1, hc], zdn),
            (aall.at[0, 0, hc], aall.at[1, 0, hc], zdn),
            (aall.at[1, 1, hc], aall.at[2, 1, hc], zdn),
            (aall.at[3, 0, hc], aall.at[3, 0, hc], sib),
            (aall.at[1, 1, hc], aall.at[1, 1, hc], sib),
            (aall.at[3, 1, hc], aall.at[3, 1, hc], sib),
            (aall.at[1, 0, hc], aall.at[1, 0, hc], sib),
            (aall.at[2, 0, hc], aall.at[2, 0, hc], sib),
            (aall.at[2, 1, hc], aall.at[2, 1, hc], sib),
        ][i]
        return remote(src, dst, a_s.at[i], a_r.at[i], dev)

    def arrived(*which):
        for i in which:
            if i == 0:
                remote(a_ref, aall.at[0, 1 - c], a_s.at[0], a_r.at[0], sib).wait_recv()
            elif i >= 7:
                r, bit = [(3, 0), (1, 1), (3, 1), (1, 0), (2, 0), (2, 1)][i - 7]
                ho = pl.ds(pl.multiple_of((1 - c) * half, half), half)
                part = aall.at[r, bit, ho]
                remote(part, part, a_s.at[i], a_r.at[i], sib).wait_recv()
            else:
                acopy(i).wait_recv()

    def begin(*which):
        for i in which:
            acopy(i).start()

    begin(0)
    aall[0, c] = a_ref[...]
    arrived(0)
    begin(1, 4, 2, 5)

    def labels(at, ends):
        total = jnp.zeros(at.shape, jnp.int32)
        for end in ends:
            total += (at >= end).astype(jnp.int32)
        return total

    def running(values):
        ends = []
        for v in values:
            ends.append(v + ends[-1] if ends else v)
        return ends

    ab_ends = running([ab_ref[h] for h in range(8)])
    chunk = 64

    def row_labels(i, _):
        at = pl.ds(pl.multiple_of(i * chunk, chunk), chunk)
        first = w * depth + i * chunk
        rowlab[at, :] = labels(first + lax.broadcasted_iota(jnp.int32, (chunk, LANES), 0), ab_ends)
        return 0

    lax.fori_loop(0, depth // chunk, row_labels, 0)
    load_b.wait()
    for s in range(2):
        cd_ends = running([cd_ref[s, h] for h in range(8)])

        def split_tile(t, _):
            first = n * cols + t * LANES
            col = labels(first + lax.broadcasted_iota(jnp.int32, (8, LANES), 1), cd_ends)[0:1]
            raw = braw[pl.ds(2 * t + s, depth, stride=2 * tiles), :]
            m = jnp.where(rowlab[...] == col, raw, 0.0)
            h = m.astype(jnp.bfloat16)
            at = pl.ds(pl.multiple_of(t * LANES, LANES), LANES)
            bh[s, :, at] = h
            bl[s, :, at] = (m - h.astype(jnp.float32)).astype(jnp.bfloat16)
            return 0

        lax.fori_loop(0, tiles, split_tile, 0)

    r_own = lax.rem(x - zh + 4, 4)
    r_last = jnp.where(r_own == 0, 2, r_own)
    r_first = jnp.where(r_own == 3, 1, 3)
    r_mid = 6 - r_last - r_first

    def slot(k):
        g = lax.div(k, 2)
        b = lax.rem(k, 2)
        r = jnp.where(g == 0, 0, jnp.where(g == 1, r_first, jnp.where(g == 2, r_mid, r_last)))
        start = jnp.where(g == 0, c, jnp.where(g == 3, 1 - zl, jnp.where(r == 3, 0, 1)))
        return r, jnp.where(b == 0, start, 1 - start)

    def slot_of(r, bit):
        found = 0
        for k in range(8):
            rk, bk = slot(k)
            found = found + jnp.where((rk == r) & (bk == bit), k, 0)
        return found

    def ring(s, t, k):
        at = lax.rem(y + 7 - t, 4) if s == 0 else lax.rem(y + 1 + t, 4)
        piece = pl.ds(pl.multiple_of(at * sub, sub), sub)
        return piece, remote(
            py.at[s, k, piece], yr.at[s, t, k], y_s.at[s, t, k], y_r.at[s, t, k],
            right if s == 0 else left,
        )

    mine = pl.ds(pl.multiple_of(y * sub, sub), sub)

    def direct(k, d):
        return remote(py.at[:, k, mine], land.at[d], d_s.at[d], d_r.at[d], owner(d))

    def sideways(k, dx, bit):
        dev = ((2 * lax.rem(x + dx, 4) + zl) * 4 + y, n)
        return remote(px.at[k], xl.at[dx, bit], x_s.at[dx, bit], x_r.at[dx, bit], dev)

    def spread(k, eb, dy):
        e = eb * 4 + dy
        piece = pl.ds(pl.multiple_of(lax.rem(y + dy, 4) * sub, sub), sub)
        return remote(px.at[k, :, piece], zl2.at[e], z_s.at[e], z_r.at[e], plane(eb, dy))

    def pass_on(t, k):
        for s in range(2):
            ring(s, t - 1, k)[1].wait_recv()
            piece, copy = ring(s, t, k)
            py[s, k, piece, :] += yr[s, t - 1, k]
            copy.start()

    def finish(k):
        for s in range(2):
            ring(s, 2, k)[1].wait_recv()
            py[s, k, mine, :] += yr[s, 2, k]
        r, bit = slot(k)
        d = lax.rem(2 * lax.rem(zh + r, 4) + bit - j + 8, 8)

        @pl.when(d != 0)
        def _():
            direct(k, d).start()

    width = 512

    def compute(k):
        r, bit = slot(k)
        a = aall[r, bit]
        ah = a.astype(jnp.bfloat16)
        ahl[0:rows] = ah
        ahl[rows:] = (a - ah.astype(jnp.float32)).astype(jnp.bfloat16)
        for s in range(2):
            for lo in range(0, cols, width):
                cs = slice(lo, lo + width)
                u = jnp.dot(ahl[...], bh[s, :, cs], preferred_element_type=jnp.float32)
                v = jnp.dot(ahl[0:rows], bl[s, :, cs], preferred_element_type=jnp.float32)
                total = u[:rows] + (u[rows:] + v)
                if lo + width <= main:
                    py[s, k, :, cs] = total
                else:
                    py[s, k, :, lo:main] = total[:, : main - lo]
                    px[k, s] = total[:, main - lo :]
            ring(s, 0, k)[1].start()
        dx = lax.rem(r - r_own + 4, 4)

        @pl.when(dx != 0)
        def _():
            sideways(k, dx, bit).start()

    def gather_side():
        for eb in range(2):
            bit = lax.rem(zl + eb, 2)
            k = slot_of(r_own, bit)
            for dx in range(1, 4):
                sideways(k, dx, bit).wait_recv()
            for dy in range(4):
                piece = pl.ds(pl.multiple_of(lax.rem(y + dy, 4) * sub, sub), sub)
                px[k, :, piece, :] += (
                    xl[1, bit, :, piece, :] + xl[2, bit, :, piece, :] + xl[3, bit, :, piece, :]
                )
                if eb + dy:
                    spread(k, eb, dy).start()

    def body(i, _):
        @pl.when(i >= 3)
        def _():
            finish(i - 3)

        @pl.when((i >= 2) & (i < 10))
        def _():
            pass_on(2, i - 2)

        @pl.when((i >= 1) & (i < 9))
        def _():
            pass_on(1, i - 1)

        @pl.when(i == 2)
        def _():
            arrived(1, 4)
            begin(3, 6, 7, 8)
            arrived(7, 8)

        @pl.when(i == 3)
        def _():
            arrived(2, 5)
            begin(9, 10)
            arrived(9, 10)

        @pl.when(i == 4)
        def _():
            arrived(3, 6)
            begin(11, 12)
            arrived(11, 12)

        @pl.when(i < 8)
        def _():
            compute(i)

        @pl.when(i == 8)
        def _():
            gather_side()

        return 0

    lax.fori_loop(0, 11, body, 0)

    k_own = slot_of(r_own, zl)
    out_ref[:, :, :main] = py[:, k_own, mine, :]
    out_ref[:, :, main:] = px[k_own, :, mine, :]
    for e in range(1, 8):
        spread(k_own, e // 4, e % 4).wait_recv()
        out_ref[:, :, main:] += zl2[e]
    for d in range(1, 8):
        direct(0, d).wait_recv()
        out_ref[:, :, :main] += land[d]
    for d in range(1, 8):
        direct(0, d).wait_send()
        spread(k_own, d // 4, d % 4).wait_send()
    for dx in range(1, 4):
        for bit in range(2):
            sideways(0, dx, bit).wait_send()
    for i in range(13):
        acopy(i).wait_send()

    def drain(k, _):
        for s in range(2):
            for t in range(3):
                ring(s, t, k)[1].wait_send()
        return 0

    lax.fori_loop(0, 8, drain, 0)


def shards(amplitudes, integrals, ab_sizes, cd_sizes):
    depth, slabs, cols = integrals.shape
    rows = amplitudes.shape[0]
    sub = rows // 4
    main = cols - SIDE
    tiles = cols // LANES
    f32 = jnp.float32
    bf16 = jnp.bfloat16
    dma = pltpu.SemaphoreType.DMA
    flat = jnp.transpose(integrals.reshape(depth, slabs, tiles, LANES), (0, 2, 1, 3))
    flat = flat.reshape(depth * tiles * slabs, LANES)
    vmem = pl.BlockSpec(memory_space=pltpu.VMEM)
    smem = pl.BlockSpec(memory_space=pltpu.SMEM)
    result = pl.pallas_call(
        ladder_kernel,
        out_shape=jax.ShapeDtypeStruct((slabs, sub, cols), f32),
        in_specs=[vmem, pl.BlockSpec(memory_space=pl.ANY), smem, smem],
        out_specs=vmem,
        scratch_shapes=[
            pltpu.VMEM((4, 2, rows, depth), f32),
            pltpu.VMEM((2 * rows, depth), bf16),
            pltpu.VMEM(flat.shape, f32),
            pltpu.VMEM((slabs, depth, cols), bf16),
            pltpu.VMEM((slabs, depth, cols), bf16),
            pltpu.VMEM((depth, LANES), jnp.int32),
            pltpu.VMEM((slabs, 8, rows, main), f32),
            pltpu.VMEM((8, slabs, rows, SIDE), f32),
            pltpu.VMEM((slabs, 3, 8, sub, main), f32),
            pltpu.VMEM((8, slabs, sub, main), f32),
            pltpu.VMEM((4, 2, slabs, rows, SIDE), f32),
            pltpu.VMEM((8, slabs, sub, SIDE), f32),
            dma(()),
            dma((13,)), dma((13,)),
            dma((slabs, 3, 8)), dma((slabs, 3, 8)),
            dma((8,)), dma((8,)),
            dma((4, 2)), dma((4, 2)),
            dma((8,)), dma((8,)),
        ],
        compiler_params=pltpu.CompilerParams(
            collective_id=0, has_side_effects=True, vmem_limit_bytes=62 * 2**20
        ),
        cost_estimate=pl.CostEstimate(
            flops=6 * 8 * rows * depth * slabs * cols, bytes_accessed=8 * 2**20, transcendentals=0
        ),
    )(amplitudes, flat, ab_sizes, cd_sizes)
    return jnp.transpose(result, (1, 0, 2))


def solution(mesh):
    return jax.shard_map(
        shards,
        mesh=mesh,
        in_specs=(P("narrow", "wide"), P("wide", None, "narrow"), P(), P()),
        out_specs=P("wide", None, "narrow"),
        check_vma=False,
    )
```

```python
import functools

import jax
import jax.numpy as jnp
from jax import lax
from jax.experimental import pallas as pl
from jax.experimental.pallas import tpu as pltpu
from jax.sharding import PartitionSpec as P

MESH = pl.DeviceIdType.MESH
LANES = 128
SIDE = 256


def ladder_kernel(
    a_ref, b_hbm, ab_ref, cd_ref, out_ref,
    aall, ahl, braw, bh, bl, rowlab, py, px, yr, xp, xl, rp, rl, zr, zl2,
    b_sem, a_s, a_r, y_s, y_r, p_s, p_r, l_s, l_r, z_s, z_r,
):
    rows, depth = a_ref.shape
    sub = rows // 4
    half = rows // 2
    cols = bh.shape[2]
    main = cols - SIDE
    tiles = cols // LANES
    w = lax.axis_index("wide")
    n = lax.axis_index("narrow")
    y = lax.rem(w, 4)
    j = lax.div(w, 4)
    x = lax.div(j, 2)
    zl = lax.rem(j, 2)
    zh = lax.div(n, 2)
    c = lax.rem(n, 2)
    right = (j * 4 + lax.rem(y + 1, 4), n)
    left = (j * 4 + lax.rem(y + 3, 4), n)
    zup = (w, lax.rem(zh + 1, 4) * 2 + c)
    zdn = (w, lax.rem(zh + 3, 4) * 2 + c)
    sib = (w, zh * 2 + 1 - c)

    xup = ((2 * lax.rem(x + 1, 4) + zl) * 4 + y, n)
    xdn = ((2 * lax.rem(x + 3, 4) + zl) * 4 + y, n)

    def plane(eb, dy):
        return ((2 * x + lax.rem(zl + eb, 2)) * 4 + lax.rem(y + dy, 4), n)

    load_b = pltpu.make_async_copy(b_hbm, braw, b_sem)
    load_b.start()

    partners = [right, left, zup, zdn, sib, xup, xdn, plane(0, 2)]
    partners += [plane(1, dy) for dy in range(4)]
    barrier = pltpu.get_barrier_semaphore()
    for dev in partners:
        pl.semaphore_signal(barrier, inc=1, device_id=dev, device_id_type=MESH)
    pl.semaphore_wait(barrier, len(partners))

    def remote(src, dst, ss, rs, dev):
        return pltpu.make_async_remote_copy(
            src_ref=src, dst_ref=dst, send_sem=ss, recv_sem=rs,
            device_id=dev, device_id_type=MESH,
        )

    hc = pl.ds(pl.multiple_of(c * half, half), half)

    def acopy(i):
        src, dst, dev = [
            (a_ref, aall.at[0, c], sib),
            (aall.at[0, 0, hc], aall.at[3, 0, hc], zup),
            (aall.at[0, 1, hc], aall.at[3, 1, hc], zup),
            (aall.at[3, 0, hc], aall.at[2, 0, hc], zup),
            (aall.at[0, 1, hc], aall.at[1, 1, hc], zdn),
            (aall.at[0, 0, hc], aall.at[1, 0, hc], zdn),
            (aall.at[1, 1, hc], aall.at[2, 1, hc], zdn),
            (aall.at[3, 0, hc], aall.at[3, 0, hc], sib),
            (aall.at[1, 1, hc], aall.at[1, 1, hc], sib),
            (aall.at[3, 1, hc], aall.at[3, 1, hc], sib),
            (aall.at[1, 0, hc], aall.at[1, 0, hc], sib),
            (aall.at[2, 0, hc], aall.at[2, 0, hc], sib),
            (aall.at[2, 1, hc], aall.at[2, 1, hc], sib),
        ][i]
        return remote(src, dst, a_s.at[i], a_r.at[i], dev)

    def arrived(*which):
        for i in which:
            if i == 0:
                remote(a_ref, aall.at[0, 1 - c], a_s.at[0], a_r.at[0], sib).wait_recv()
            elif i >= 7:
                r, bit = [(3, 0), (1, 1), (3, 1), (1, 0), (2, 0), (2, 1)][i - 7]
                ho = pl.ds(pl.multiple_of((1 - c) * half, half), half)
                part = aall.at[r, bit, ho]
                remote(part, part, a_s.at[i], a_r.at[i], sib).wait_recv()
            else:
                acopy(i).wait_recv()

    def begin(*which):
        for i in which:
            acopy(i).start()

    begin(0)
    aall[0, c] = a_ref[...]
    arrived(0)
    begin(1, 4)

    def labels(at, ends):
        total = jnp.zeros(at.shape, jnp.int32)
        for end in ends:
            total += (at >= end).astype(jnp.int32)
        return total

    def running(values):
        ends = []
        for v in values:
            ends.append(v + ends[-1] if ends else v)
        return ends

    ab_ends = running([ab_ref[h] for h in range(8)])
    chunk = 64

    def row_labels(i, _):
        at = pl.ds(pl.multiple_of(i * chunk, chunk), chunk)
        first = w * depth + i * chunk
        rowlab[at, :] = labels(first + lax.broadcasted_iota(jnp.int32, (chunk, LANES), 0), ab_ends)
        return 0

    lax.fori_loop(0, depth // chunk, row_labels, 0)
    def split_slab(s):
        cd_ends = running([cd_ref[s, h] for h in range(8)])

        def split_tile(t, _):
            first = n * cols + t * LANES
            col = labels(first + lax.broadcasted_iota(jnp.int32, (8, LANES), 1), cd_ends)[0:1]
            raw = braw[pl.ds(2 * t + s, depth, stride=2 * tiles), :]
            m = jnp.where(rowlab[...] == col, raw, 0.0)
            h = m.astype(jnp.bfloat16)
            at = pl.ds(pl.multiple_of(t * LANES, LANES), LANES)
            bh[s, :, at] = h
            bl[s, :, at] = (m - h.astype(jnp.float32)).astype(jnp.bfloat16)
            return 0

        lax.fori_loop(0, tiles, split_tile, 0)

    r_own = lax.rem(x - zh + 4, 4)

    def slot(k):
        far = (k == 5) | (k == 7)
        near = (k == 3) | (k == 4)
        r = jnp.where(k < 2, 0, jnp.where(far, 2, jnp.where(near, 1, 3)))
        bit = jnp.where(near, 4 - k, lax.div(k, 4))
        bit = jnp.where(far, jnp.where(k == 7, zl, 1 - zl), bit)
        return r, jnp.where(k < 2, lax.rem(k + c, 2), bit)

    def slot_of(r, bit):
        found = 0
        for k in range(8):
            rk, bk = slot(k)
            found = found + jnp.where((rk == r) & (bk == bit), k, 0)
        return found

    def ring(s, t, k):
        at = lax.rem(y + 7 - t, 4) if s == 0 else lax.rem(y + 1 + t, 4)
        piece = pl.ds(pl.multiple_of(at * sub, sub), sub)
        return piece, remote(
            py.at[s, k, piece], yr.at[s, t, k], y_s.at[s, t, k], y_r.at[s, t, k],
            right if s == 0 else left,
        )

    mine = pl.ds(pl.multiple_of(y * sub, sub), sub)

    def data(kind, k, s):
        return py.at[s, k, mine] if kind else px.at[k, s]

    def handed(kind, k, e, bit):
        dst = (rp if kind else xp).at[e, bit]
        sems = p_s.at[kind, e, bit], p_r.at[kind, e, bit]
        return remote(data(kind, k, e), dst, *sems, xdn if e else xup)

    def landing(kind, k, f, bit, s):
        dst = (rl if kind else xl).at[f, bit, s]
        sems = l_s.at[kind, f, bit, s], l_r.at[kind, f, bit, s]
        return remote(data(kind, k, s), dst, *sems, xdn if f else xup)

    def towards(k):
        r, bit = slot(k)
        return lax.rem(r - r_own + 4, 4), bit

    def hand_out(kind, k):
        dx, bit = towards(k)

        @pl.when(dx == 2)
        def _():
            for e in range(2):
                handed(kind, k, e, bit).start()

        for f in range(2):
            @pl.when(dx == 1 + 2 * f)
            def _():
                landing(kind, k, f, bit, 1 - f).start()

    def relay(kind, k):
        dx, bit = towards(k)
        for f in range(2):
            @pl.when(dx == 1 + 2 * f)
            def _():
                handed(kind, k, f, bit).wait_recv()
                if kind:
                    py[f, k, mine, :] += rp[f, bit]
                else:
                    px[k, f] += xp[f, bit]
                landing(kind, k, f, bit, f).start()

    def landed(kind, k, bit):
        for f in range(2):
            for s in range(2):
                landing(kind, k, f, bit, s).wait_recv()

    def across(k):
        return remote(py.at[:, k, mine], zr, z_s.at[0], z_r.at[0], plane(1, 0))

    def collect(k):
        dx, bit = towards(k)

        @pl.when(dx == 0)
        def _():
            landed(1, k, bit)
            for s in range(2):
                py[s, k, mine, :] += rl[0, bit, s] + rl[1, bit, s]

            @pl.when(bit != zl)
            def _():
                across(k).start()

    def spread(k, eb, dy):
        e = eb * 4 + dy
        piece = pl.ds(pl.multiple_of(lax.rem(y + dy, 4) * sub, sub), sub)
        return remote(px.at[k, :, piece], zl2.at[e], z_s.at[e], z_r.at[e], plane(eb, dy))

    def pass_on(t, k):
        for s in range(2):
            ring(s, t - 1, k)[1].wait_recv()
            piece, copy = ring(s, t, k)
            py[s, k, piece, :] += yr[s, t - 1, k]
            copy.start()

    def finish(k):
        for s in range(2):
            ring(s, 2, k)[1].wait_recv()
            py[s, k, mine, :] += yr[s, 2, k]
        hand_out(1, k)

    width = 512

    def split_rows(k):
        r, bit = slot(k)
        a = aall[r, bit]
        ah = a.astype(jnp.bfloat16)
        ahl[0:rows] = ah
        ahl[rows:] = (a - ah.astype(jnp.float32)).astype(jnp.bfloat16)

    def compute_slab(k, s):
        for lo in range(0, cols, width):
            cs = slice(lo, lo + width)
            u = jnp.dot(ahl[...], bh[s, :, cs], preferred_element_type=jnp.float32)
            v = jnp.dot(ahl[0:rows], bl[s, :, cs], preferred_element_type=jnp.float32)
            total = u[:rows] + (u[rows:] + v)
            if lo + width <= main:
                py[s, k, :, cs] = total
            else:
                py[s, k, :, lo:main] = total[:, : main - lo]
                px[k, s] = total[:, main - lo :]

    def compute(k):
        split_rows(k)
        for s in range(2):
            compute_slab(k, s)
        hand_out(0, k)

    def gather_side(k):
        dx, bit = towards(k)

        @pl.when(dx == 0)
        def _():
            landed(0, k, bit)
            eb = lax.rem(bit - zl + 2, 2)
            for dy in range(4):
                piece = pl.ds(pl.multiple_of(lax.rem(y + dy, 4) * sub, sub), sub)
                px[k, :, piece, :] += xl[0, bit, :, piece, :] + xl[1, bit, :, piece, :]
                if dy:
                    spread(k, eb, dy).start()
                else:
                    @pl.when(eb != 0)
                    def _():
                        spread(k, eb, 0).start()

    def send_first(k):
        for s in range(2):
            ring(s, 0, k)[1].start()

    split_rows(0)
    load_b.wait()
    for s in range(2):
        split_slab(s)
        compute_slab(0, s)
        ring(s, 0, 0)[1].start()
    hand_out(0, 0)

    def body(i, _):
        def stages(*which):
            for late, what in which:
                @pl.when((i >= late) & (i < late + 8))
                def _():
                    what(i - late)

        @pl.when((i > 0) & (i < 8))
        def _():
            send_first(i)

        @pl.when(i != 2)
        def _():
            stages(
                (1, functools.partial(pass_on, 1)),
                (2, functools.partial(pass_on, 2)),
            )

        stages((3, finish))

        @pl.when(i == 1)
        def _():
            pass_on(1, 1)
            acopy(1).wait_send()
            begin(2)
            acopy(4).wait_send()
            begin(5)
            pass_on(2, 0)
            arrived(1, 4)
            begin(3, 6, 7, 8)
            arrived(7, 8)

        @pl.when(i == 3)
        def _():
            arrived(2, 5)
            begin(9, 10)
            arrived(9, 10)

        @pl.when(i == 4)
        def _():
            arrived(3, 6)
            begin(11, 12)
            arrived(11, 12)

        stages(
            (-1, compute),
            (1, functools.partial(relay, 0)),
            (4, functools.partial(relay, 1)),
            (3, gather_side),
            (5, collect),
        )
        return 0

    lax.fori_loop(0, 13, body, 0)

    k_own = slot_of(r_own, zl)
    out_ref[:, :, :main] = py[:, k_own, mine, :]
    out_ref[:, :, main:] = px[k_own, :, mine, :]
    for e in range(1, 8):
        spread(k_own, e // 4, e % 4).wait_recv()
        out_ref[:, :, main:] += zl2[e]
    across(k_own).wait_recv()
    out_ref[:, :, :main] += zr[...]
    across(k_own).wait_send()
    for e in range(1, 8):
        spread(k_own, e // 4, e % 4).wait_send()
    for kind in range(2):
        for f in range(2):
            for bit in range(2):
                handed(kind, 0, f, bit).wait_send()
                for s in range(2):
                    landing(kind, 0, f, bit, s).wait_send()
    for i in (0, 2, 3) + tuple(range(5, 13)):
        acopy(i).wait_send()

    def drain(k, _):
        for s in range(2):
            for t in range(3):
                ring(s, t, k)[1].wait_send()
        return 0

    lax.fori_loop(0, 8, drain, 0)


def shards(amplitudes, integrals, ab_sizes, cd_sizes):
    depth, slabs, cols = integrals.shape
    rows = amplitudes.shape[0]
    sub = rows // 4
    main = cols - SIDE
    tiles = cols // LANES
    f32 = jnp.float32
    bf16 = jnp.bfloat16
    dma = pltpu.SemaphoreType.DMA
    flat = jnp.transpose(integrals.reshape(depth, slabs, tiles, LANES), (0, 2, 1, 3))
    flat = flat.reshape(depth * tiles * slabs, LANES)
    vmem = pl.BlockSpec(memory_space=pltpu.VMEM)
    smem = pl.BlockSpec(memory_space=pltpu.SMEM)
    result = pl.pallas_call(
        ladder_kernel,
        out_shape=jax.ShapeDtypeStruct((slabs, sub, cols), f32),
        in_specs=[vmem, pl.BlockSpec(memory_space=pl.ANY), smem, smem],
        out_specs=vmem,
        scratch_shapes=[
            pltpu.VMEM((4, 2, rows, depth), f32),
            pltpu.VMEM((2 * rows, depth), bf16),
            pltpu.VMEM(flat.shape, f32),
            pltpu.VMEM((slabs, depth, cols), bf16),
            pltpu.VMEM((slabs, depth, cols), bf16),
            pltpu.VMEM((depth, LANES), jnp.int32),
            pltpu.VMEM((slabs, 8, rows, main), f32),
            pltpu.VMEM((8, slabs, rows, SIDE), f32),
            pltpu.VMEM((slabs, 3, 8, sub, main), f32),
            pltpu.VMEM((2, 2, rows, SIDE), f32),
            pltpu.VMEM((2, 2, slabs, rows, SIDE), f32),
            pltpu.VMEM((2, 2, sub, main), f32),
            pltpu.VMEM((2, 2, slabs, sub, main), f32),
            pltpu.VMEM((slabs, sub, main), f32),
            pltpu.VMEM((8, slabs, sub, SIDE), f32),
            dma(()),
            dma((13,)), dma((13,)),
            dma((slabs, 3, 8)), dma((slabs, 3, 8)),
            dma((2, 2, 2)), dma((2, 2, 2)),
            dma((2, 2, 2, 2)), dma((2, 2, 2, 2)),
            dma((8,)), dma((8,)),
        ],
        compiler_params=pltpu.CompilerParams(
            collective_id=0, has_side_effects=True, vmem_limit_bytes=62 * 2**20
        ),
        cost_estimate=pl.CostEstimate(
            flops=6 * 8 * rows * depth * slabs * cols, bytes_accessed=8 * 2**20, transcendentals=0
        ),
    )(amplitudes, flat, ab_sizes, cd_sizes)
    return jnp.transpose(result, (1, 0, 2))


def solution(mesh):
    return jax.shard_map(
        shards,
        mesh=mesh,
        in_specs=(P("narrow", "wide"), P("wide", None, "narrow"), P(), P()),
        out_specs=P("wide", None, "narrow"),
        check_vma=False,
    )
```

```python
import functools

import jax
import jax.numpy as jnp
from jax import lax
from jax.experimental import pallas as pl
from jax.experimental.pallas import tpu as pltpu
from jax.sharding import PartitionSpec as P

MESH = pl.DeviceIdType.MESH
LANES = 128
SIDE = 256


def ladder_kernel(
    a_ref, b_hbm, ab_ref, cd_ref, out_ref,
    aall, ahl, braw, bh, bl, rowlab, py, px, yr, xp, xl, rp, rl, zr, zl2,
    b_sem, a_s, a_r, y_s, y_r, p_s, p_r, l_s, l_r, z_s, z_r,
):
    rows, depth = a_ref.shape
    sub = rows // 4
    half = rows // 2
    cols = bh.shape[2]
    main = cols - SIDE
    tiles = cols // LANES
    w = lax.axis_index("wide")
    n = lax.axis_index("narrow")
    y = lax.rem(w, 4)
    j = lax.div(w, 4)
    x = lax.div(j, 2)
    zl = lax.rem(j, 2)
    zh = lax.div(n, 2)
    c = lax.rem(n, 2)
    right = (j * 4 + lax.rem(y + 1, 4), n)
    left = (j * 4 + lax.rem(y + 3, 4), n)
    zup = (w, lax.rem(zh + 1, 4) * 2 + c)
    zdn = (w, lax.rem(zh + 3, 4) * 2 + c)
    sib = (w, zh * 2 + 1 - c)

    xup = ((2 * lax.rem(x + 1, 4) + zl) * 4 + y, n)
    xdn = ((2 * lax.rem(x + 3, 4) + zl) * 4 + y, n)

    def plane(eb, dy):
        return ((2 * x + lax.rem(zl + eb, 2)) * 4 + lax.rem(y + dy, 4), n)

    load_b = pltpu.make_async_copy(b_hbm, braw, b_sem)
    load_b.start()

    partners = [right, left, zup, zdn, sib, xup, xdn, plane(0, 2)]
    partners += [plane(1, dy) for dy in range(4)]
    barrier = pltpu.get_barrier_semaphore()
    for dev in partners:
        pl.semaphore_signal(barrier, inc=1, device_id=dev, device_id_type=MESH)
    pl.semaphore_wait(barrier, len(partners))

    def remote(src, dst, ss, rs, dev):
        return pltpu.make_async_remote_copy(
            src_ref=src, dst_ref=dst, send_sem=ss, recv_sem=rs,
            device_id=dev, device_id_type=MESH,
        )

    hc = pl.ds(pl.multiple_of(c * half, half), half)

    def acopy(i):
        src, dst, dev = [
            (a_ref, aall.at[0, c], sib),
            (aall.at[0, 0, hc], aall.at[3, 0, hc], zup),
            (aall.at[0, 1, hc], aall.at[3, 1, hc], zup),
            (aall.at[3, 0, hc], aall.at[2, 0, hc], zup),
            (aall.at[0, 1, hc], aall.at[1, 1, hc], zdn),
            (aall.at[0, 0, hc], aall.at[1, 0, hc], zdn),
            (aall.at[1, 1, hc], aall.at[2, 1, hc], zdn),
            (aall.at[3, 0, hc], aall.at[3, 0, hc], sib),
            (aall.at[1, 1, hc], aall.at[1, 1, hc], sib),
            (aall.at[3, 1, hc], aall.at[3, 1, hc], sib),
            (aall.at[1, 0, hc], aall.at[1, 0, hc], sib),
            (aall.at[2, 0, hc], aall.at[2, 0, hc], sib),
            (aall.at[2, 1, hc], aall.at[2, 1, hc], sib),
        ][i]
        return remote(src, dst, a_s.at[i], a_r.at[i], dev)

    def arrived(*which):
        for i in which:
            if i == 0:
                remote(a_ref, aall.at[0, 1 - c], a_s.at[0], a_r.at[0], sib).wait_recv()
            elif i >= 7:
                r, bit = [(3, 0), (1, 1), (3, 1), (1, 0), (2, 0), (2, 1)][i - 7]
                ho = pl.ds(pl.multiple_of((1 - c) * half, half), half)
                part = aall.at[r, bit, ho]
                remote(part, part, a_s.at[i], a_r.at[i], sib).wait_recv()
            else:
                acopy(i).wait_recv()

    def begin(*which):
        for i in which:
            acopy(i).start()

    begin(0)
    aall[0, c] = a_ref[...]
    arrived(0)
    begin(1, 4)

    def labels(at, ends):
        total = jnp.zeros(at.shape, jnp.int32)
        for end in ends:
            total += (at >= end).astype(jnp.int32)
        return total

    def running(values):
        ends = []
        for v in values:
            ends.append(v + ends[-1] if ends else v)
        return ends

    ab_ends = running([ab_ref[h] for h in range(8)])
    chunk = 64

    def row_labels(i, _):
        at = pl.ds(pl.multiple_of(i * chunk, chunk), chunk)
        first = w * depth + i * chunk
        rowlab[at, :] = labels(first + lax.broadcasted_iota(jnp.int32, (chunk, LANES), 0), ab_ends)
        return 0

    lax.fori_loop(0, depth // chunk, row_labels, 0)
    def split_slab(s):
        cd_ends = running([cd_ref[s, h] for h in range(8)])

        def split_tile(t, _):
            first = n * cols + t * LANES
            col = labels(first + lax.broadcasted_iota(jnp.int32, (8, LANES), 1), cd_ends)[0:1]
            raw = braw[pl.ds(2 * t + s, depth, stride=2 * tiles), :]
            m = jnp.where(rowlab[...] == col, raw, 0.0)
            h = m.astype(jnp.bfloat16)
            at = pl.ds(pl.multiple_of(t * LANES, LANES), LANES)
            bh[s, :, at] = h
            bl[s, :, at] = (m - h.astype(jnp.float32)).astype(jnp.bfloat16)
            return 0

        lax.fori_loop(0, tiles, split_tile, 0)

    r_own = lax.rem(x - zh + 4, 4)

    def slot(k):
        far = (k == 5) | (k == 7)
        up = (k == 3) | (k == 6)
        r = jnp.where(k < 2, 0, jnp.where(far, 2, jnp.where(up, 1, 3)))
        bit = jnp.where(up, jnp.where(k == 3, 1, 0), lax.div(k, 4))
        bit = jnp.where(far, jnp.where(k == 7, zl, 1 - zl), bit)
        return r, jnp.where(k < 2, lax.rem(k + c, 2), bit)

    def slot_of(r, bit):
        found = 0
        for k in range(8):
            rk, bk = slot(k)
            found = found + jnp.where((rk == r) & (bk == bit), k, 0)
        return found

    def ring(s, t, k):
        at = lax.rem(y + 7 - t, 4) if s == 0 else lax.rem(y + 1 + t, 4)
        piece = pl.ds(pl.multiple_of(at * sub, sub), sub)
        return piece, remote(
            py.at[s, k, piece], yr.at[s, t, k], y_s.at[s, t, k], y_r.at[s, t, k],
            right if s == 0 else left,
        )

    mine = pl.ds(pl.multiple_of(y * sub, sub), sub)

    def data(kind, k, s):
        return py.at[s, k, mine] if kind else px.at[k, s]

    def handed(kind, k, e, bit):
        dst = (rp if kind else xp).at[e, bit]
        sems = p_s.at[kind, e, bit], p_r.at[kind, e, bit]
        return remote(data(kind, k, e), dst, *sems, xdn if e else xup)

    def landing(kind, k, f, bit, s):
        dst = (rl if kind else xl).at[f, bit, s]
        sems = l_s.at[kind, f, bit, s], l_r.at[kind, f, bit, s]
        return remote(data(kind, k, s), dst, *sems, xdn if f else xup)

    def towards(k):
        r, bit = slot(k)
        return lax.rem(r - r_own + 4, 4), bit

    def hand_out(kind, k):
        dx, bit = towards(k)

        @pl.when(dx == 2)
        def _():
            for e in range(2):
                handed(kind, k, e, bit).start()

        for f in range(2):
            @pl.when(dx == 1 + 2 * f)
            def _():
                landing(kind, k, f, bit, 1 - f).start()

    def relay(kind, k):
        dx, bit = towards(k)
        for f in range(2):
            @pl.when(dx == 1 + 2 * f)
            def _():
                handed(kind, k, f, bit).wait_recv()
                if kind:
                    py[f, k, mine, :] += rp[f, bit]
                else:
                    px[k, f] += xp[f, bit]
                landing(kind, k, f, bit, f).start()

    def landed(kind, k, bit):
        for f in range(2):
            for s in range(2):
                landing(kind, k, f, bit, s).wait_recv()

    def across(k):
        return remote(py.at[:, k, mine], zr, z_s.at[0], z_r.at[0], plane(1, 0))

    def collect(k):
        dx, bit = towards(k)

        @pl.when(dx == 0)
        def _():
            landed(1, k, bit)
            for s in range(2):
                py[s, k, mine, :] += rl[0, bit, s] + rl[1, bit, s]

            @pl.when(bit != zl)
            def _():
                across(k).start()

    def spread(k, eb, dy):
        e = eb * 4 + dy
        piece = pl.ds(pl.multiple_of(lax.rem(y + dy, 4) * sub, sub), sub)
        return remote(px.at[k, :, piece], zl2.at[e], z_s.at[e], z_r.at[e], plane(eb, dy))

    def pass_on(t, k):
        for s in range(2):
            ring(s, t - 1, k)[1].wait_recv()
            piece, copy = ring(s, t, k)
            py[s, k, piece, :] += yr[s, t - 1, k]
            copy.start()

    def finish(k):
        for s in range(2):
            ring(s, 2, k)[1].wait_recv()
            py[s, k, mine, :] += yr[s, 2, k]
        hand_out(1, k)

    width = 512

    def split_rows(k):
        r, bit = slot(k)
        a = aall[r, bit]
        ah = a.astype(jnp.bfloat16)
        ahl[0:rows] = ah
        ahl[rows:] = (a - ah.astype(jnp.float32)).astype(jnp.bfloat16)

    def compute_slab(k, s):
        for lo in range(0, cols, width):
            cs = slice(lo, lo + width)
            u = jnp.dot(ahl[...], bh[s, :, cs], preferred_element_type=jnp.float32)
            v = jnp.dot(ahl[0:rows], bl[s, :, cs], preferred_element_type=jnp.float32)
            total = u[:rows] + (u[rows:] + v)
            if lo + width <= main:
                py[s, k, :, cs] = total
            else:
                py[s, k, :, lo:main] = total[:, : main - lo]
                px[k, s] = total[:, main - lo :]

    def compute(k):
        split_rows(k)
        for s in range(2):
            compute_slab(k, s)
        hand_out(0, k)

    def gather_side(k):
        dx, bit = towards(k)

        @pl.when(dx == 0)
        def _():
            landed(0, k, bit)
            eb = lax.rem(bit - zl + 2, 2)
            for dy in range(4):
                piece = pl.ds(pl.multiple_of(lax.rem(y + dy, 4) * sub, sub), sub)
                px[k, :, piece, :] += xl[0, bit, :, piece, :] + xl[1, bit, :, piece, :]
                if dy:
                    spread(k, eb, dy).start()
                else:
                    @pl.when(eb != 0)
                    def _():
                        spread(k, eb, 0).start()

    def send_first(k):
        for s in range(2):
            ring(s, 0, k)[1].start()

    split_rows(0)
    load_b.wait()
    for s in range(2):
        split_slab(s)
        compute_slab(0, s)
        ring(s, 0, 0)[1].start()
    hand_out(0, 0)

    def body(i, _):
        def stages(*which):
            for late, what in which:
                @pl.when((i >= late) & (i < late + 8))
                def _():
                    what(i - late)

        @pl.when((i > 0) & (i < 8))
        def _():
            send_first(i)

        @pl.when(i != 2)
        def _():
            stages(
                (1, functools.partial(pass_on, 1)),
                (2, functools.partial(pass_on, 2)),
            )

        stages((3, finish))

        stages(
            (1, functools.partial(relay, 0)),
            (4, functools.partial(relay, 1)),
            (3, gather_side),
            (5, collect),
        )

        @pl.when(i == 1)
        def _():
            pass_on(1, 1)
            acopy(1).wait_send()
            begin(2)
            acopy(4).wait_send()
            begin(5)
            pass_on(2, 0)
            arrived(1, 4)
            begin(3, 6, 7, 8)
            arrived(7, 8)

        @pl.when(i == 3)
        def _():
            arrived(2, 5)
            begin(9, 10)
            arrived(9, 10)

        @pl.when(i == 4)
        def _():
            arrived(3, 6)
            begin(11, 12)
            arrived(11, 12)

        stages((-1, compute))
        return 0

    lax.fori_loop(0, 13, body, 0)

    k_own = slot_of(r_own, zl)
    out_ref[:, :, :main] = py[:, k_own, mine, :]
    out_ref[:, :, main:] = px[k_own, :, mine, :]
    for e in range(1, 8):
        spread(k_own, e // 4, e % 4).wait_recv()
        out_ref[:, :, main:] += zl2[e]
    across(k_own).wait_recv()
    out_ref[:, :, :main] += zr[...]
    across(k_own).wait_send()
    for e in range(1, 8):
        spread(k_own, e // 4, e % 4).wait_send()
    for kind in range(2):
        for f in range(2):
            for bit in range(2):
                handed(kind, 0, f, bit).wait_send()
                for s in range(2):
                    landing(kind, 0, f, bit, s).wait_send()
    for i in (0, 2, 3) + tuple(range(5, 13)):
        acopy(i).wait_send()

    def drain(k, _):
        for s in range(2):
            for t in range(3):
                ring(s, t, k)[1].wait_send()
        return 0

    lax.fori_loop(0, 8, drain, 0)


def shards(amplitudes, integrals, ab_sizes, cd_sizes):
    depth, slabs, cols = integrals.shape
    rows = amplitudes.shape[0]
    sub = rows // 4
    main = cols - SIDE
    tiles = cols // LANES
    f32 = jnp.float32
    bf16 = jnp.bfloat16
    dma = pltpu.SemaphoreType.DMA
    flat = jnp.transpose(integrals.reshape(depth, slabs, tiles, LANES), (0, 2, 1, 3))
    flat = flat.reshape(depth * tiles * slabs, LANES)
    vmem = pl.BlockSpec(memory_space=pltpu.VMEM)
    smem = pl.BlockSpec(memory_space=pltpu.SMEM)
    result = pl.pallas_call(
        ladder_kernel,
        out_shape=jax.ShapeDtypeStruct((slabs, sub, cols), f32),
        in_specs=[vmem, pl.BlockSpec(memory_space=pl.ANY), smem, smem],
        out_specs=vmem,
        scratch_shapes=[
            pltpu.VMEM((4, 2, rows, depth), f32),
            pltpu.VMEM((2 * rows, depth), bf16),
            pltpu.VMEM(flat.shape, f32),
            pltpu.VMEM((slabs, depth, cols), bf16),
            pltpu.VMEM((slabs, depth, cols), bf16),
            pltpu.VMEM((depth, LANES), jnp.int32),
            pltpu.VMEM((slabs, 8, rows, main), f32),
            pltpu.VMEM((8, slabs, rows, SIDE), f32),
            pltpu.VMEM((slabs, 3, 8, sub, main), f32),
            pltpu.VMEM((2, 2, rows, SIDE), f32),
            pltpu.VMEM((2, 2, slabs, rows, SIDE), f32),
            pltpu.VMEM((2, 2, sub, main), f32),
            pltpu.VMEM((2, 2, slabs, sub, main), f32),
            pltpu.VMEM((slabs, sub, main), f32),
            pltpu.VMEM((8, slabs, sub, SIDE), f32),
            dma(()),
            dma((13,)), dma((13,)),
            dma((slabs, 3, 8)), dma((slabs, 3, 8)),
            dma((2, 2, 2)), dma((2, 2, 2)),
            dma((2, 2, 2, 2)), dma((2, 2, 2, 2)),
            dma((8,)), dma((8,)),
        ],
        compiler_params=pltpu.CompilerParams(
            collective_id=0, has_side_effects=True, vmem_limit_bytes=62 * 2**20
        ),
        cost_estimate=pl.CostEstimate(
            flops=6 * 8 * rows * depth * slabs * cols, bytes_accessed=8 * 2**20, transcendentals=0
        ),
    )(amplitudes, flat, ab_sizes, cd_sizes)
    return jnp.transpose(result, (1, 0, 2))


def solution(mesh):
    return jax.shard_map(
        shards,
        mesh=mesh,
        in_specs=(P("narrow", "wide"), P("wide", None, "narrow"), P(), P()),
        out_specs=P("wide", None, "narrow"),
        check_vma=False,
    )
```

```python
import functools

import jax
import jax.numpy as jnp
from jax import lax
from jax.experimental import pallas as pl
from jax.experimental.pallas import tpu as pltpu
from jax.sharding import PartitionSpec as P

MESH = pl.DeviceIdType.MESH
LANES = 128
SIDE = 256


def ladder_kernel(
    a_ref, b_hbm, ab_ref, cd_ref, out_ref, acc,
    aall, ahl, braw, bh, bl, rowlab, py, px, yr, xp, xl, rp, rl, zr, zl2,
    b_sem, a_s, a_r, y_s, y_r, p_s, p_r, l_s, l_r, z_s, z_r,
):
    rows, depth = a_ref.shape
    sub = rows // 4
    half = rows // 2
    cols = bh.shape[2]
    main = cols - SIDE
    tiles = cols // LANES
    w = lax.axis_index("wide")
    n = lax.axis_index("narrow")
    y = lax.rem(w, 4)
    j = lax.div(w, 4)
    x = lax.div(j, 2)
    zl = lax.rem(j, 2)
    zh = lax.div(n, 2)
    c = lax.rem(n, 2)
    right = (j * 4 + lax.rem(y + 1, 4), n)
    left = (j * 4 + lax.rem(y + 3, 4), n)
    zup = (w, lax.rem(zh + 1, 4) * 2 + c)
    zdn = (w, lax.rem(zh + 3, 4) * 2 + c)
    sib = (w, zh * 2 + 1 - c)

    xup = ((2 * lax.rem(x + 1, 4) + zl) * 4 + y, n)
    xdn = ((2 * lax.rem(x + 3, 4) + zl) * 4 + y, n)

    def plane(eb, dy):
        return ((2 * x + lax.rem(zl + eb, 2)) * 4 + lax.rem(y + dy, 4), n)

    load_b = pltpu.make_async_copy(b_hbm, braw, b_sem)
    load_b.start()

    partners = [right, left, zup, zdn, sib, xup, xdn, plane(0, 2)]
    partners += [plane(1, dy) for dy in range(4)]
    barrier = pltpu.get_barrier_semaphore()
    for dev in partners:
        pl.semaphore_signal(barrier, inc=1, device_id=dev, device_id_type=MESH)
    pl.semaphore_wait(barrier, len(partners))

    def remote(src, dst, ss, rs, dev):
        return pltpu.make_async_remote_copy(
            src_ref=src, dst_ref=dst, send_sem=ss, recv_sem=rs,
            device_id=dev, device_id_type=MESH,
        )

    hc = pl.ds(pl.multiple_of(c * half, half), half)

    def acopy(i):
        src, dst, dev = [
            (a_ref, aall.at[0, c], sib),
            (aall.at[0, 0, hc], aall.at[3, 0, hc], zup),
            (aall.at[0, 1, hc], aall.at[3, 1, hc], zup),
            (aall.at[3, 0, hc], aall.at[2, 0, hc], zup),
            (aall.at[0, 1, hc], aall.at[1, 1, hc], zdn),
            (aall.at[0, 0, hc], aall.at[1, 0, hc], zdn),
            (aall.at[1, 1, hc], aall.at[2, 1, hc], zdn),
            (aall.at[3, 0, hc], aall.at[3, 0, hc], sib),
            (aall.at[1, 1, hc], aall.at[1, 1, hc], sib),
            (aall.at[3, 1, hc], aall.at[3, 1, hc], sib),
            (aall.at[1, 0, hc], aall.at[1, 0, hc], sib),
            (aall.at[2, 0, hc], aall.at[2, 0, hc], sib),
            (aall.at[2, 1, hc], aall.at[2, 1, hc], sib),
        ][i]
        return remote(src, dst, a_s.at[i], a_r.at[i], dev)

    def arrived(*which):
        for i in which:
            if i == 0:
                remote(a_ref, aall.at[0, 1 - c], a_s.at[0], a_r.at[0], sib).wait_recv()
            elif i >= 7:
                r, bit = [(3, 0), (1, 1), (3, 1), (1, 0), (2, 0), (2, 1)][i - 7]
                ho = pl.ds(pl.multiple_of((1 - c) * half, half), half)
                part = aall.at[r, bit, ho]
                remote(part, part, a_s.at[i], a_r.at[i], sib).wait_recv()
            else:
                acopy(i).wait_recv()

    def begin(*which):
        for i in which:
            acopy(i).start()

    begin(0)
    aall[0, c] = a_ref[...]
    arrived(0)
    begin(1, 4)

    def labels(at, ends):
        total = jnp.zeros(at.shape, jnp.int32)
        for end in ends:
            total += (at >= end).astype(jnp.int32)
        return total

    def running(values):
        ends = []
        for v in values:
            ends.append(v + ends[-1] if ends else v)
        return ends

    ab_ends = running([ab_ref[h] for h in range(8)])
    chunk = 64

    def row_labels(i, _):
        at = pl.ds(pl.multiple_of(i * chunk, chunk), chunk)
        first = w * depth + i * chunk
        rowlab[at, :] = labels(first + lax.broadcasted_iota(jnp.int32, (chunk, LANES), 0), ab_ends)
        return 0

    lax.fori_loop(0, depth // chunk, row_labels, 0)
    def split_slab(s):
        cd_ends = running([cd_ref[s, h] for h in range(8)])

        def split_tile(t, _):
            first = n * cols + t * LANES
            col = labels(first + lax.broadcasted_iota(jnp.int32, (8, LANES), 1), cd_ends)[0:1]
            raw = braw[pl.ds(2 * t + s, depth, stride=2 * tiles), :]
            m = jnp.where(rowlab[...] == col, raw, 0.0)
            h = m.astype(jnp.bfloat16)
            at = pl.ds(pl.multiple_of(t * LANES, LANES), LANES)
            bh[s, :, at] = h
            bl[s, :, at] = (m - h.astype(jnp.float32)).astype(jnp.bfloat16)
            return 0

        lax.fori_loop(0, tiles, split_tile, 0)

    r_own = lax.rem(x - zh + 4, 4)

    def slot(k):
        far = (k == 5) | (k == 7)
        up = (k == 3) | (k == 6)
        r = jnp.where(k < 2, 0, jnp.where(far, 2, jnp.where(up, 1, 3)))
        bit = jnp.where(up, jnp.where(k == 3, 1, 0), lax.div(k, 4))
        bit = jnp.where(far, jnp.where(k == 7, zl, 1 - zl), bit)
        return r, jnp.where(k < 2, lax.rem(k + c, 2), bit)

    def slot_of(r, bit):
        found = 0
        for k in range(8):
            rk, bk = slot(k)
            found = found + jnp.where((rk == r) & (bk == bit), k, 0)
        return found

    def ring(s, t, k):
        at = lax.rem(y + 7 - t, 4) if s == 0 else lax.rem(y + 1 + t, 4)
        piece = pl.ds(pl.multiple_of(at * sub, sub), sub)
        return piece, remote(
            py.at[s, k, piece], yr.at[s, t, k], y_s.at[s, t, k], y_r.at[s, t, k],
            right if s == 0 else left,
        )

    mine = pl.ds(pl.multiple_of(y * sub, sub), sub)

    def data(kind, k, s):
        return py.at[s, k, mine] if kind else px.at[k, s]

    def handed(kind, k, e, bit):
        dst = (rp if kind else xp).at[e, bit]
        sems = p_s.at[kind, e, bit], p_r.at[kind, e, bit]
        return remote(data(kind, k, e), dst, *sems, xdn if e else xup)

    def landing(kind, k, f, bit, s):
        dst = (rl if kind else xl).at[f, bit, s]
        sems = l_s.at[kind, f, bit, s], l_r.at[kind, f, bit, s]
        return remote(data(kind, k, s), dst, *sems, xdn if f else xup)

    def towards(k):
        r, bit = slot(k)
        return lax.rem(r - r_own + 4, 4), bit

    def hand_out(kind, k):
        dx, bit = towards(k)

        @pl.when(dx == 2)
        def _():
            for e in range(2):
                handed(kind, k, e, bit).start()

        for f in range(2):
            @pl.when(dx == 1 + 2 * f)
            def _():
                landing(kind, k, f, bit, 1 - f).start()

    def relay(kind, k):
        dx, bit = towards(k)
        for f in range(2):
            @pl.when(dx == 1 + 2 * f)
            def _():
                handed(kind, k, f, bit).wait_recv()
                if kind:
                    py[f, k, mine, :] += rp[f, bit]
                else:
                    px[k, f] += xp[f, bit]
                landing(kind, k, f, bit, f).start()

    def landed(kind, k, bit):
        for f in range(2):
            for s in range(2):
                landing(kind, k, f, bit, s).wait_recv()

    def across(k):
        return remote(py.at[:, k, mine], zr, z_s.at[0], z_r.at[0], plane(1, 0))

    def collect(k):
        dx, bit = towards(k)

        @pl.when(dx == 0)
        def _():
            landed(1, k, bit)
            for s in range(2):
                py[s, k, mine, :] += rl[0, bit, s] + rl[1, bit, s]

            @pl.when(bit != zl)
            def _():
                across(k).start()

    def spread(k, eb, dy):
        e = eb * 4 + dy
        piece = pl.ds(pl.multiple_of(lax.rem(y + dy, 4) * sub, sub), sub)
        return remote(px.at[k, :, piece], zl2.at[e], z_s.at[e], z_r.at[e], plane(eb, dy))

    def pass_on(t, k):
        for s in range(2):
            ring(s, t - 1, k)[1].wait_recv()
            piece, copy = ring(s, t, k)
            py[s, k, piece, :] += yr[s, t - 1, k]
            copy.start()

    def finish(k):
        for s in range(2):
            ring(s, 2, k)[1].wait_recv()
            py[s, k, mine, :] += yr[s, 2, k]
        hand_out(1, k)

    width = 512

    def split_rows(k):
        r, bit = slot(k)
        a = aall[r, bit]
        ah = a.astype(jnp.bfloat16)
        ahl[0:rows] = ah
        ahl[rows:] = (a - ah.astype(jnp.float32)).astype(jnp.bfloat16)

    def compute_slab(k, s):
        for lo in range(0, cols, width):
            cs = slice(lo, lo + width)
            u = jnp.dot(ahl[...], bh[s, :, cs], preferred_element_type=jnp.float32)
            v = jnp.dot(ahl[0:rows], bl[s, :, cs], preferred_element_type=jnp.float32)
            total = u[:rows] + (u[rows:] + v)
            if lo + width <= main:
                py[s, k, :, cs] = total
            else:
                py[s, k, :, lo:main] = total[:, : main - lo]
                px[k, s] = total[:, main - lo :]

    def compute(k):
        split_rows(k)
        for s in range(2):
            compute_slab(k, s)
        hand_out(0, k)

    def gather_side(k):
        dx, bit = towards(k)

        @pl.when(dx == 0)
        def _():
            landed(0, k, bit)
            eb = lax.rem(bit - zl + 2, 2)
            for dy in range(4):
                piece = pl.ds(pl.multiple_of(lax.rem(y + dy, 4) * sub, sub), sub)
                px[k, :, piece, :] += xl[0, bit, :, piece, :] + xl[1, bit, :, piece, :]
                if dy:
                    spread(k, eb, dy).start()
                else:
                    @pl.when(eb != 0)
                    def _():
                        spread(k, eb, 0).start()

    def send_first(k):
        for s in range(2):
            ring(s, 0, k)[1].start()

    split_rows(0)
    load_b.wait()
    for s in range(2):
        split_slab(s)
        compute_slab(0, s)
        ring(s, 0, 0)[1].start()
    hand_out(0, 0)

    def body(i, _):
        def stages(*which):
            for late, what in which:
                @pl.when((i >= late) & (i < late + 8))
                def _():
                    what(i - late)

        @pl.when((i > 0) & (i < 8))
        def _():
            send_first(i)

        @pl.when(i != 2)
        def _():
            stages(
                (1, functools.partial(pass_on, 1)),
                (2, functools.partial(pass_on, 2)),
            )

        stages((3, finish))

        stages(
            (1, functools.partial(relay, 0)),
            (4, functools.partial(relay, 1)),
            (3, gather_side),
            (5, collect),
        )

        @pl.when(i == 1)
        def _():
            pass_on(1, 1)
            acopy(1).wait_send()
            begin(2)
            acopy(4).wait_send()
            begin(5)
            pass_on(2, 0)
            arrived(1, 4)
            begin(3, 6, 7, 8)
            arrived(7, 8)

        @pl.when(i == 3)
        def _():
            arrived(2, 5)
            begin(9, 10)
            arrived(9, 10)

        @pl.when(i == 4)
        def _():
            arrived(3, 6)
            begin(11, 12)
            arrived(11, 12)

        stages((-1, compute))
        return 0

    lax.fori_loop(0, 13, body, 0)

    k_own = slot_of(r_own, zl)
    acc[:, :, :main] = py[:, k_own, mine, :]
    acc[:, :, main:] = px[k_own, :, mine, :]
    for e in range(1, 8):
        spread(k_own, e // 4, e % 4).wait_recv()
        acc[:, :, main:] += zl2[e]
    across(k_own).wait_recv()
    acc[:, :, :main] += zr[...]
    for s in range(2):
        for t in range(tiles):
            lane = slice(t * LANES, (t + 1) * LANES)
            out_ref[pl.ds(2 * t + s, sub, stride=2 * tiles), :] = acc[s, :, lane]
    across(k_own).wait_send()
    for e in range(1, 8):
        spread(k_own, e // 4, e % 4).wait_send()
    for kind in range(2):
        for f in range(2):
            for bit in range(2):
                handed(kind, 0, f, bit).wait_send()
                for s in range(2):
                    landing(kind, 0, f, bit, s).wait_send()
    for i in (0, 2, 3) + tuple(range(5, 13)):
        acopy(i).wait_send()

    def drain(k, _):
        for s in range(2):
            for t in range(3):
                ring(s, t, k)[1].wait_send()
        return 0

    lax.fori_loop(0, 8, drain, 0)


def shards(amplitudes, integrals, ab_sizes, cd_sizes):
    depth, slabs, cols = integrals.shape
    rows = amplitudes.shape[0]
    sub = rows // 4
    main = cols - SIDE
    tiles = cols // LANES
    f32 = jnp.float32
    bf16 = jnp.bfloat16
    dma = pltpu.SemaphoreType.DMA
    flat = jnp.transpose(integrals.reshape(depth, slabs, tiles, LANES), (0, 2, 1, 3))
    flat = flat.reshape(depth * tiles * slabs, LANES)
    vmem = pl.BlockSpec(memory_space=pltpu.VMEM)
    smem = pl.BlockSpec(memory_space=pltpu.SMEM)
    result = pl.pallas_call(
        ladder_kernel,
        out_shape=jax.ShapeDtypeStruct((sub * tiles * slabs, LANES), f32),
        in_specs=[vmem, pl.BlockSpec(memory_space=pl.ANY), smem, smem],
        out_specs=vmem,
        scratch_shapes=[
            pltpu.VMEM((slabs, sub, cols), f32),
            pltpu.VMEM((4, 2, rows, depth), f32),
            pltpu.VMEM((2 * rows, depth), bf16),
            pltpu.VMEM(flat.shape, f32),
            pltpu.VMEM((slabs, depth, cols), bf16),
            pltpu.VMEM((slabs, depth, cols), bf16),
            pltpu.VMEM((depth, LANES), jnp.int32),
            pltpu.VMEM((slabs, 8, rows, main), f32),
            pltpu.VMEM((8, slabs, rows, SIDE), f32),
            pltpu.VMEM((slabs, 3, 8, sub, main), f32),
            pltpu.VMEM((2, 2, rows, SIDE), f32),
            pltpu.VMEM((2, 2, slabs, rows, SIDE), f32),
            pltpu.VMEM((2, 2, sub, main), f32),
            pltpu.VMEM((2, 2, slabs, sub, main), f32),
            pltpu.VMEM((slabs, sub, main), f32),
            pltpu.VMEM((8, slabs, sub, SIDE), f32),
            dma(()),
            dma((13,)), dma((13,)),
            dma((slabs, 3, 8)), dma((slabs, 3, 8)),
            dma((2, 2, 2)), dma((2, 2, 2)),
            dma((2, 2, 2, 2)), dma((2, 2, 2, 2)),
            dma((8,)), dma((8,)),
        ],
        compiler_params=pltpu.CompilerParams(
            collective_id=0, has_side_effects=True, vmem_limit_bytes=62 * 2**20
        ),
        cost_estimate=pl.CostEstimate(
            flops=6 * 8 * rows * depth * slabs * cols, bytes_accessed=8 * 2**20, transcendentals=0
        ),
    )(amplitudes, flat, ab_sizes, cd_sizes)
    result = jnp.transpose(result.reshape(sub, tiles, slabs, LANES), (0, 2, 1, 3))
    return result.reshape(sub, slabs, cols)


def solution(mesh):
    return jax.shard_map(
        shards,
        mesh=mesh,
        in_specs=(P("narrow", "wide"), P("wide", None, "narrow"), P(), P()),
        out_specs=P("wide", None, "narrow"),
        check_vma=False,
    )
```
